1024 devices in a mesh: fsdp: 128 (over y, z_lo, core), island: 8 (over z_hi, x).
Axes of the slice: x: 4, y: 8, z: 16 (z_hi: 2, z_lo: 8; z = z_hi * 8 + z_lo), core: 2. Of those that a mesh axis runs over, the one named last changes fastest.
Arguments:
- context: bfloat16 [5120, 2048], P('fsdp', 'island'), may hold values from -6 to 6
- cotangent: bfloat16 [5120, 2048], P('fsdp', 'island'), may hold values from -6 to 6
- weights: float32 [8, 5120, 5120], P('island', 'fsdp'), may hold values from -0.3125 to 0.3125
- moment_one: bfloat16 [8, 5120, 5120], P('island', 'fsdp'), may hold values from -60 to 60
- moment_two: bfloat16 [8, 5120, 5120], P('island', 'fsdp'), may hold values from 10 to 400
- outer: float32 [5120, 5120], P('fsdp'), may hold values from -0.078125 to 0.078125
- momentum: float32 [5120, 5120], P('fsdp'), may hold values from -0.12 to 0.12
- step: int32 [1], replicated, may hold values from 0 to 4095
- plan: int32 [40], replicated, may hold values from 0 to 3, as said below
Outputs:
- layer_out: bfloat16 [5120, 2048], P('fsdp', 'island')
- context_grad: bfloat16 [5120, 2048], P('fsdp', 'island')
- weights_out: float32 [8, 5120, 5120], P('island', 'fsdp')
- outer_new: float32 [5120, 5120], P('fsdp')
- momentum_new: float32 [5120, 5120], P('fsdp')
The draws below stay inside these ranges and needn't reach their ends.
Inputs may be any that keep to these rules, and one draw needn't show every extreme that they name: `plan`: each of the 4 fragment numbers names exactly 10 blocks.
All inputs are finite; a program needn't handle non-finite values.
Results may differ from the reference program's by a relative error of at most 0.0095.
Values may be sent and summed in bfloat16 or wider, within the bound.
A program may use at most 32 MiB of HBM per device.

```python
import math
import jax
import jax.numpy as jnp

K = 5120
N = 5120
TOKENS = 256
FRAGMENTS = 4
SLABS = 40
N_ISLAND = 8


def draw_plan(key, part):
    key = jax.random.fold_in(key, 7)
    shuffled = jax.random.permutation(key, SLABS)
    return (shuffled % FRAGMENTS).astype(jnp.int32)


def strengthened(drawn, stream_key, source, target, shards_of, factor):
    owner, partner = [(jnp.arange(drawn.shape[position]) // (drawn.shape[position] // shards_of)).reshape([-1 if axis == position else 1 for axis in range(drawn.ndim)]) for position in (source, target)]
    chosen = jax.random.permutation(stream_key, shards_of)[partner]
    strong = (owner == chosen) | (owner == (partner + shards_of // 2) % shards_of)
    return jnp.where(strong, factor * drawn, drawn)


def levels(own_key, shape, pieces, least, largest):
    level, own = 1.0, jax.random.fold_in(own_key, 6)
    for position, shards_of in pieces:
        draws = jnp.exp(jax.random.uniform(jax.random.fold_in(own, position), (shards_of,), jnp.float32, least / len(pieces), largest / len(pieces)))
        level = level * jnp.repeat(draws, shape[position] // shards_of).reshape([-1 if axis == position else 1 for axis in range(len(shape))])
    return level


def noise(stream_key, dims, deviation, limit, cuts=(), dtype=jnp.bfloat16):
    result = jax.random.normal(stream_key, dims, jnp.float32) * deviation
    if len(cuts) > 0:
        result = levels(stream_key, dims, cuts, -0.22, 0.18) * result
    return jnp.clip(result, min=-limit, max=limit).astype(dtype)


def bell_draw_with(stream_key, extent, scale, limit, cuts, heavy, kind=jnp.bfloat16):
    drawn = scale * jax.random.normal(stream_key, extent, jnp.float32)
    if cuts:
        drawn = drawn * levels(stream_key, extent, cuts, -0.22, 0.18)
    return jnp.clip(strengthened(drawn, jax.random.fold_in(stream_key, 3), *heavy), -limit, limit).astype(kind)


def setup_inputs(seed: int = 0) -> dict:
    streams_of = jax.random.split(jax.random.key(seed), 10)
    return {
        "context": noise(streams_of[0], (K, N_ISLAND * TOKENS), 1.0, 6.0, ((0, 128), (1, 8))),
        "cotangent": noise(streams_of[1], (N, N_ISLAND * TOKENS), 1.0, 6.0, ((0, 128), (1, 8))),
        "weights": bell_draw_with(streams_of[2], (N_ISLAND, K, N), K ** -0.5, 0.3125, ((0, 8), (1, 128)), (1, 2, 128, 5.5), jnp.float32),
        "moment_one": noise(streams_of[3], (N_ISLAND, K, N), 10.0, 60.0, ((0, 8), (1, 128))),
        "moment_two": jnp.clip(jnp.exp(math.log(400.0) - 3.6888795 * jax.random.uniform(streams_of[4], (N_ISLAND, K, N), jnp.float32) ** levels(streams_of[4], (N_ISLAND, K, N), ((0, 8), (1, 128)), -0.2, 0.2)), 10.0, 400.0).astype(jnp.bfloat16),
        "outer": noise(streams_of[5], (K, N), K ** -0.5, 0.078125, ((0, 128),), jnp.float32),
        "momentum": noise(streams_of[6], (K, N), 0.02, 0.12, ((0, 128),), jnp.float32),
        "step": jax.random.randint(streams_of[7], (1,), 0, 4096).astype(jnp.int32),
        "plan": draw_plan(jax.random.fold_in(streams_of[9], 71), 0),
    }


beta_one = 0.9
beta_two = 0.95
inner_rate = 0.01
weight_decay = 0.1
epsilon = 1e-08
outer_rate = 0.7
momentum_keep = 0.9
period_steps = 4096.0

def reference(context, cotangent, weights, moment_one, moment_two, outer, momentum, step, plan):
    current = step[0] % FRAGMENTS
    rate = inner_rate * (0.55 + 0.45 * jnp.cos(math.pi * step[0].astype(jnp.float32) / period_steps))
    matched = plan == current
    column_mask = jnp.repeat(matched, 128)[None, :]
    outputs = []
    inputs_grad = []
    stepped_all = []
    total = jnp.zeros(outer.shape, jnp.float32)
    for island in range(N_ISLAND):
        first_row = island * TOKENS
        activations = context[:, first_row:first_row + TOKENS]
        incoming = cotangent[:, first_row:first_row + TOKENS]
        master = weights[island]
        weight_half = master.astype(jnp.bfloat16)
        outputs.append(jnp.dot(weight_half.T, activations, preferred_element_type=jnp.float32).astype(jnp.bfloat16))
        inputs_grad.append(jnp.dot(weight_half, incoming, preferred_element_type=jnp.float32).astype(jnp.bfloat16))
        weight_grad = jnp.dot(activations, incoming.T, preferred_element_type=jnp.float32)
        first = beta_one * moment_one[island].astype(jnp.float32) + (1.0 - beta_one) * weight_grad
        second = beta_two * moment_two[island].astype(jnp.float32) + (1.0 - beta_two) * weight_grad * weight_grad
        stepped = master - rate * (first / (jnp.sqrt(second) + epsilon) + weight_decay * master)
        stepped_all.append(stepped)
        total = total + (outer - stepped)
    pseudo_grad = total / N_ISLAND
    momentum_new = jnp.where(column_mask, momentum_keep * momentum + pseudo_grad, momentum)
    outer_new = jnp.where(column_mask, outer - outer_rate * (pseudo_grad + momentum_keep * momentum_new), outer)
    weights_out = jnp.stack([jnp.where(column_mask, outer_new, stepped) for stepped in stepped_all])
    return (jnp.concatenate(outputs, axis=1), jnp.concatenate(inputs_grad, axis=1), weights_out, outer_new, momentum_new)
```

```python
import functools
import math

import jax
import jax.numpy as jnp
from jax import lax
from jax.experimental import pallas as pl
from jax.experimental.pallas import tpu as pltpu
from jax.sharding import PartitionSpec as P

FRAGMENTS = 4

beta_one = 0.9
beta_two = 0.95
inner_rate = 0.01
weight_decay = 0.1
epsilon = 1e-08
outer_rate = 0.7
momentum_keep = 0.9
period_steps = 4096.0

NY, NZ, NX = 8, 8, 4
ROWS = 40
PAD = 48
UNIT = 80
CHUNK = NZ * UNIT
TOK = 256
HALF = 128
BLOCKS = 40
CHOSEN = 10
QUARTER = 112

f32 = jnp.float32
bf16 = jnp.bfloat16
MESH = pl.DeviceIdType.MESH


def loop(count, body):
    def step(i, carry):
        body(i)
        return carry

    lax.fori_loop(0, count, step, 0)


def exchange_kernel(
    step_s,
    plan_s,
    rate_s,
    ctx_h,
    cot_h,
    w_h,
    m1_h,
    m2_h,
    outer_h,
    lo_o,
    cg_o,
    stepped_o,
    sync_o,
    ctx_v,
    cot_v,
    w_v,
    m1_v,
    m2_v,
    outer_v,
    cots,
    chip80,
    ctxs,
    ctx96,
    ctxp,
    w96,
    coth,
    part,
    rr,
    rl,
    sr,
    sl,
    zbuf,
    zrec,
    acc,
    diff,
    gath,
    xs,
    xr,
    zhs,
    zhr,
    fin,
    keep,
    given,
    in_sem,
    sib_s,
    sib_r,
    chs,
    chr_,
    azs,
    azr,
    ars,
    arr,
    als,
    alr,
    rrs,
    rrr,
    rls,
    rlr,
    rzs,
    rzr,
    xss,
    xsr,
    zh_s,
    zh_r,
    xas,
    xar,
):
    fs = lax.axis_index("fsdp")
    isl = lax.axis_index("island")
    c = lax.rem(fs, 2)
    o = 1 - c
    z = lax.rem(lax.div(fs, 2), NZ)
    y = lax.div(fs, 2 * NZ)
    x = lax.rem(isl, NX)
    zh = lax.div(isl, NX)

    def ymod(v):
        return lax.rem(v + 2 * NY, NY)

    def dev(yy, zz, cc):
        return ((yy * NZ + zz) * 2 + cc, isl)

    sibling = (y * NZ * 2 + z * 2 + o, isl)
    right = dev(ymod(y + 1), z, c)
    left = dev(ymod(y - 1), z, c)

    def zdev(d):
        return dev(y, lax.rem(z + d, NZ), c)

    def xdev(d):
        return (fs, zh * NX + lax.rem(x + d, NX))

    zhdev = (fs, (1 - zh) * NX + x)

    def remote(src, dst, send, recv, device):
        return pltpu.make_async_remote_copy(
            src_ref=src,
            dst_ref=dst,
            send_sem=send,
            recv_sem=recv,
            device_id=device,
            device_id_type=MESH,
        )

    loads = [
        pltpu.make_async_copy(src, dst, in_sem.at[i])
        for i, (src, dst) in enumerate(
            (
                (cot_h, cot_v),
                (ctx_h, ctx_v),
                (w_h, w_v),
                (m1_h, m1_v),
                (m2_h, m2_v),
                (outer_h, outer_v),
            )
        )
    ]
    for load in loads:
        load.start()

    barrier = pltpu.get_barrier_semaphore()

    def greet(device):
        pl.semaphore_signal(barrier, inc=1, device_id=device, device_id_type=MESH)

    greet(sibling)
    greet(right)
    greet(left)
    for d in range(1, NZ):
        greet(zdev(d))
    for d in range(1, NX):
        greet(xdev(d))
    greet(zhdev)
    pl.semaphore_wait(barrier, 3 + NZ - 1 + NX - 1 + 1)

    mine40 = pl.ds(pl.multiple_of(c * ROWS, 8), ROWS)
    other40 = pl.ds(pl.multiple_of(o * ROWS, 8), ROWS)
    mine48 = pl.ds(pl.multiple_of(c * PAD, 16), PAD)
    other48 = pl.ds(pl.multiple_of(o * PAD, 16), PAD)

    loads[0].wait()
    for h in range(2):
        cots[h] = cot_v[:, h * HALF : (h + 1) * HALF].astype(f32)
    sib_cot = remote(cots.at[o], chip80.at[mine40], sib_s.at[0], sib_r.at[0], sibling)
    sib_cot.start()
    chip80[mine40, :] = cots[c]

    loads[1].wait()
    wide = jnp.concatenate([ctx_v[...].astype(f32), jnp.zeros((PAD - ROWS, TOK), f32)], axis=0)
    wide = wide.astype(bf16)
    ctxp[...] = wide
    for h in range(2):
        ctxs[h] = wide[:, h * HALF : (h + 1) * HALF]
    sib_ctx = remote(ctxs.at[o], ctx96.at[mine48], sib_s.at[1], sib_r.at[1], sibling)
    sib_ctx.start()
    ctx96[mine48, :] = ctxs[c]

    def d_of(p):
        return lax.rem(
            lax.rem(p, 2) * lax.div(p + 1, 2) + (1 - lax.rem(p, 2)) * (NZ - lax.div(p, 2)), NZ
        )

    def ag_z_send(d):
        ref = coth.at[c, y, z]
        return remote(ref, ref, azs.at[d], azr.at[d], zdev(d))

    def ag_z_recv(d):
        ref = coth.at[c, y, lax.rem(z + NZ - d, NZ)]
        return remote(ref, ref, azs.at[d], azr.at[d], zdev(d))

    def ag_y(s, p, sign, landed):
        unit = lax.rem(z + d_of(p), NZ)
        ref = coth.at[c, ymod(y - sign * (s + landed)), unit]
        if sign > 0:
            return remote(ref, ref, ars.at[s, p], arr.at[s, p], right)
        return remote(ref, ref, als.at[s, p], alr.at[s, p], left)

    def chunk_copy(k, yc):
        ref = coth.at[c, yc]
        return remote(ref, ref, chs.at[k], chr_.at[k], sibling)

    def chunk_recv(k, yc):
        ref = coth.at[o, yc]
        return remote(ref, ref, chs.at[k], chr_.at[k], sibling)

    remote(cots.at[o], chip80.at[other40], sib_s.at[0], sib_r.at[0], sibling).wait_recv()
    coth[c, y, z] = chip80[...].astype(bf16)

    def z_send(i):
        ag_z_send(d_of(i + 1)).start()

    loop(NZ - 1, z_send)
    ag_y(0, 0, 1, 0).start()
    ag_y(0, 0, -1, 0).start()

    loads[2].wait()

    def half_weights(i):
        lanes = pl.ds(pl.multiple_of(i * CHUNK, 128), CHUNK)
        rows = jnp.concatenate([w_v[:, lanes], jnp.zeros((PAD - ROWS, CHUNK), f32)], axis=0)
        w96[mine48, lanes] = rows.astype(bf16)

    loop(NY, half_weights)
    sib_w = remote(w96.at[mine48], w96.at[mine48], sib_s.at[2], sib_r.at[2], sibling)
    sib_w.start()

    def first_units(lo, hi):
        def body(i):
            p = i + lo
            ag_z_recv(lax.rem(NZ - d_of(p), NZ)).wait_recv()
            ag_y(0, p, 1, 0).start()
            ag_y(0, p, -1, 0).start()

        loop(hi - lo, body)

    first_units(1, 3)

    remote(ctxs.at[o], ctx96.at[other48], sib_s.at[1], sib_r.at[1], sibling).wait_recv()
    remote(w96.at[mine48], w96.at[other48], sib_s.at[2], sib_r.at[2], sibling).wait_recv()

    def partial_out(i):
        lanes = pl.ds(pl.multiple_of(i * CHUNK, 128), CHUNK)
        total = lax.dot_general(
            w96[:, lanes], ctx96[...], (((0,), (0,)), ((), ())), preferred_element_type=f32
        )
        part[i] = total.reshape(NZ, UNIT, HALF)

    loop(NY, partial_out)

    def rs_d(g, q):
        return lax.rem(3 + 4 * g + q, NZ)

    def rs_copy(s, j, sign):
        if sign > 0:
            return remote(sr.at[s, j], rr.at[s, j], rrs.at[s, j], rrr.at[s, j], right)
        return remote(sl.at[s, j], rl.at[s, j], rls.at[s, j], rlr.at[s, j], left)

    def rs_step(g, s):
        def body(q2):
            for parity in range(2):
                q = 2 * q2 + parity
                j = 4 * g + q
                u = lax.rem(z + rs_d(g, q), NZ)
                for sign, hops in ((1, 4 - parity), (-1, 3 + parity)):
                    if s < hops:
                        value = part[ymod(y + sign * (hops - s)), u]
                        if s > 0:
                            rs_copy(s - 1, j, sign).wait_recv()
                            came = rr if sign > 0 else rl
                            value = value + came[s - 1, j].astype(f32)
                        going = sr if sign > 0 else sl
                        going[s, j] = value.astype(bf16)
                        rs_copy(s, j, sign).start()

        loop(2, body)

    def rs_z(j, d):
        return remote(zbuf.at[j], zrec.at[j], rzs.at[j], rzr.at[j], zdev(d))

    def rs_last(g):
        def body(q2):
            for parity in range(2):
                q = 2 * q2 + parity
                j = 4 * g + q
                d = rs_d(g, q)
                rs_copy(3 - parity, j, 1).wait_recv()
                rs_copy(2 + parity, j, -1).wait_recv()
                value = part[y, lax.rem(z + d, NZ)]
                value = value + rr[3 - parity, j].astype(f32) + rl[2 + parity, j].astype(f32)
                if parity == 1 and g == 1:

                    @pl.when(q2 == 0)
                    def _():
                        keep[...] = value

                    @pl.when(q2 != 0)
                    def _():
                        zbuf[j] = value.astype(bf16)
                        rs_z(j, d).start()

                else:
                    zbuf[j] = value.astype(bf16)
                    rs_z(j, d).start()

        loop(2, body)

    rs_step(0, 0)
    first_units(3, 5)
    rs_step(1, 0)
    first_units(5, NZ)
    chunk_copy(0, y).start()

    acc[...] = jnp.zeros_like(acc)
    rate = rate_s[0]

    def compute(k, yc):
        chunk_recv(k, yc).wait_recv()
        lanes = pl.ds(pl.multiple_of(yc * CHUNK, 128), CHUNK)
        incoming = jnp.concatenate(
            [coth[0, yc].reshape(CHUNK, HALF), coth[1, yc].reshape(CHUNK, HALF)], axis=1
        )
        acc[...] += jnp.dot(w96[mine48, lanes], incoming, preferred_element_type=f32)
        grad = lax.dot_general(
            ctxp[...], incoming, (((1,), (1,)), ((), ())), preferred_element_type=f32
        )[:ROWS]
        master = w_v[:, lanes]
        first = beta_one * m1_v[:, lanes].astype(f32) + (1.0 - beta_one) * grad
        second = beta_two * m2_v[:, lanes].astype(f32) + (1.0 - beta_two) * grad * grad
        stepped = master - rate * (first / (jnp.sqrt(second) + epsilon) + weight_decay * master)
        stepped_o[:, lanes] = stepped
        delta = outer_v[:, lanes] - stepped
        for b in range(CHUNK // HALF):
            diff[yc * (CHUNK // HALF) + b] = delta[:, b * HALF : (b + 1) * HALF]

    def compute_pair(s):
        def body(i):
            compute(2 * s - 1 + i, ymod(y + (2 * i - 1) * s))

        loop(2, body)

    def share_pair(s):
        chunk_copy(2 * s - 1, ymod(y - s)).start()
        chunk_copy(2 * s, ymod(y + s)).start()

    def ag_forward(s):
        def body(p2):
            for parity in range(2):
                p = 2 * p2 + parity
                for sign, hops in ((1, 4 - parity), (-1, 3 + parity)):
                    ag_y(s - 1, p, sign, 1).wait_recv()
                    if s < hops:
                        ag_y(s, p, sign, 0).start()

        loop(NZ // 2, body)

    ag_forward(1)
    share_pair(1)
    for i in range(3, 6):
        loads[i].wait()
    compute(0, y)
    ag_forward(2)
    share_pair(2)
    compute_pair(1)
    ag_forward(3)
    share_pair(3)
    rs_step(0, 1)
    compute_pair(2)

    def ag_end(p2):
        ag_y(3, 2 * p2, 1, 1).wait_recv()
        ag_y(3, 2 * p2 + 1, -1, 1).wait_recv()

    loop(NZ // 2, ag_end)
    chunk_copy(7, ymod(y + 4)).start()
    rs_step(0, 2)
    compute_pair(3)
    rs_step(1, 1)
    compute(7, ymod(y + 4))

    current = lax.rem(step_s[0], FRAGMENTS)

    def rank(b, carry):
        count, found = carry[0], carry[1:]
        hit = plan_s[b] == current
        found = tuple(jnp.where(hit & (count == i), b, e) for i, e in enumerate(found))
        return (count + hit.astype(jnp.int32),) + found

    ranked = lax.fori_loop(0, BLOCKS, rank, (jnp.int32(0),) * (CHOSEN + 1))
    chosen = ranked[1:]
    for i in range(CHOSEN):
        gath[i * ROWS : (i + 1) * ROWS, :] = diff[chosen[i]]
    gath[CHOSEN * ROWS :, :] = jnp.zeros((NX * QUARTER - CHOSEN * ROWS, HALF), f32)
    xs[...] = gath[...].astype(bf16).reshape(NX, QUARTER, HALF)

    def x_scatter(d):
        return remote(xs.at[lax.rem(x + d, NX)], xr.at[d], xss.at[d], xsr.at[d], xdev(d))

    def x_gather(d):
        return remote(fin.at[x], fin.at[x], xas.at[d], xar.at[d], xdev(d))

    def x_gathered(d):
        ref = fin.at[lax.rem(x + NX - d, NX)]
        return remote(ref, ref, xas.at[d], xar.at[d], xdev(d))

    for d in range(1, NX):
        x_scatter(d).start()
    rs_step(0, 3)
    rs_step(1, 2)
    for d in range(1, NX):
        x_scatter(d).wait_recv()
    total = xs[x].astype(f32)
    for d in range(1, NX):
        total = total + xr[d].astype(f32)
    zhs[...] = total.astype(bf16)
    across = remote(zhs, zhr, zh_s, zh_r, zhdev)
    across.start()
    rs_last(0)
    rs_step(1, 3)
    across.wait_recv()
    fin[x] = (zhs[...].astype(f32) + zhr[...].astype(f32)).astype(bf16)
    for d in range(1, NX):
        x_gather(d).start()
    rs_last(1)
    cg_o[...] = acc[:ROWS, :]
    for d in range(1, NX):
        x_gathered(d).wait_recv()
    sync_o[...] = fin[...].reshape(NX * QUARTER, HALF).astype(f32)

    value = keep[...]
    for j in (0, 1, 2, 3, 4, 6, 7):
        rs_z(j, (3 + j) % NZ).wait_recv()
        value = value + zrec[j].astype(f32)
    keep[...] = value
    give = remote(keep.at[other40], given, sib_s.at[3], sib_r.at[3], sibling)
    give.start()
    lo_o[c] = keep[mine40, :]
    give.wait_recv()
    lo_o[o] = given[...]

    give.wait_send()
    sib_cot.wait_send()
    sib_ctx.wait_send()
    sib_w.wait_send()
    loop(NZ - 1, lambda i: ag_z_send(d_of(i + 1)).wait_send())

    def ag_sent(p2):
        for parity in range(2):
            p = 2 * p2 + parity
            for sign, hops in ((1, 4 - parity), (-1, 3 + parity)):
                for s in range(hops):
                    ag_y(s, p, sign, 0).wait_send()

    loop(NZ // 2, ag_sent)
    chunk_copy(0, y).wait_send()
    for s in range(1, 4):
        chunk_copy(2 * s - 1, ymod(y - s)).wait_send()
        chunk_copy(2 * s, ymod(y + s)).wait_send()
    chunk_copy(7, ymod(y + 4)).wait_send()

    def rs_sent(j2):
        for parity in range(2):
            j = 2 * j2 + parity
            for sign, hops in ((1, 4 - parity), (-1, 3 + parity)):
                for s in range(hops):
                    rs_copy(s, j, sign).wait_send()

    loop(NZ // 2, rs_sent)
    for j in (0, 1, 2, 3, 4, 6, 7):
        rs_z(j, (3 + j) % NZ).wait_send()
    for d in range(1, NX):
        x_scatter(d).wait_send()
        x_gather(d).wait_send()
    across.wait_send()


GRID = 4


def apply_kernel(
    step_s,
    plan_s,
    lo_i,
    cg_i,
    sync_i,
    stepped_i,
    outer_i,
    mom_i,
    lo_o,
    cg_o,
    w_o,
    outer_o,
    mom_o,
):
    tile = pl.program_id(0)
    per = BLOCKS // GRID

    @pl.when(tile == 0)
    def _():
        for h in range(2):
            lo_o[:, h * HALF : (h + 1) * HALF] = lo_i[h].astype(bf16)
        cg_o[...] = cg_i[...].astype(bf16)

    current = lax.rem(step_s[0], FRAGMENTS)

    def before(b, count):
        return count + (plan_s[b] == current).astype(jnp.int32)

    count = lax.fori_loop(0, tile * per, before, jnp.int32(0))
    for b in range(per):
        lanes = slice(b * HALF, (b + 1) * HALF)
        hit = plan_s[tile * per + b] == current
        slot = jnp.minimum(count, CHOSEN - 1)
        pseudo = sync_i[pl.ds(pl.multiple_of(slot * ROWS, 8), ROWS), :] / 8.0
        count = count + hit.astype(jnp.int32)
        old, mom = outer_i[:, lanes], mom_i[:, lanes]
        mom_next = momentum_keep * mom + pseudo
        new = old - outer_rate * (pseudo + momentum_keep * mom_next)
        mom_o[:, lanes] = jnp.where(hit, mom_next, mom)
        outer_o[:, lanes] = jnp.where(hit, new, old)
        w_o[:, lanes] = jnp.where(hit, new, stepped_i[:, lanes])


def per_device(context, cotangent, weights, moment_one, moment_two, outer, momentum, step, plan):
    n = outer.shape[1]
    rate = inner_rate * (0.55 + 0.45 * jnp.cos(math.pi * step.astype(f32) / period_steps))
    smem = pl.BlockSpec(memory_space=pltpu.SMEM)
    vmem = pl.BlockSpec(memory_space=pltpu.VMEM)
    hbm = pl.BlockSpec(memory_space=pltpu.HBM)
    dma = pltpu.SemaphoreType.DMA
    steps = (4, NZ)
    lo, cg, stepped, sync = pl.pallas_call(
        exchange_kernel,
        out_shape=(
            jax.ShapeDtypeStruct((2, ROWS, HALF), f32),
            jax.ShapeDtypeStruct((ROWS, TOK), f32),
            jax.ShapeDtypeStruct((ROWS, n), f32),
            jax.ShapeDtypeStruct((NX * QUARTER, HALF), f32),
        ),
        in_specs=[smem] * 3 + [hbm] * 6,
        out_specs=(vmem,) * 4,
        scratch_shapes=[
            pltpu.VMEM((ROWS, TOK), bf16),
            pltpu.VMEM((ROWS, TOK), bf16),
            pltpu.VMEM((ROWS, n), f32),
            pltpu.VMEM((ROWS, n), bf16),
            pltpu.VMEM((ROWS, n), bf16),
            pltpu.VMEM((ROWS, n), f32),
            pltpu.VMEM((2, ROWS, HALF), f32),
            pltpu.VMEM((UNIT, HALF), f32),
            pltpu.VMEM((2, PAD, HALF), bf16),
            pltpu.VMEM((2 * PAD, HALF), bf16),
            pltpu.VMEM((PAD, TOK), bf16),
            pltpu.VMEM((2 * PAD, n), bf16),
            pltpu.VMEM((2, NY, NZ, UNIT, HALF), bf16),
            pltpu.VMEM((NY, NZ, UNIT, HALF), f32),
            pltpu.VMEM(steps + (UNIT, HALF), bf16),
            pltpu.VMEM(steps + (UNIT, HALF), bf16),
            pltpu.VMEM(steps + (UNIT, HALF), bf16),
            pltpu.VMEM(steps + (UNIT, HALF), bf16),
            pltpu.VMEM((NZ, UNIT, HALF), bf16),
            pltpu.VMEM((NZ, UNIT, HALF), bf16),
            pltpu.VMEM((PAD, TOK), f32),
            pltpu.VMEM((BLOCKS, ROWS, HALF), f32),
            pltpu.VMEM((NX * QUARTER, HALF), f32),
            pltpu.VMEM((NX, QUARTER, HALF), bf16),
            pltpu.VMEM((NX, QUARTER, HALF), bf16),
            pltpu.VMEM((QUARTER, HALF), bf16),
            pltpu.VMEM((QUARTER, HALF), bf16),
            pltpu.VMEM((NX, QUARTER, HALF), bf16),
            pltpu.VMEM((UNIT, HALF), f32),
            pltpu.VMEM((ROWS, HALF), f32),
            dma((6,)),
            dma((4,)),
            dma((4,)),
            dma((NY,)),
            dma((NY,)),
            dma((NZ,)),
            dma((NZ,)),
            dma(steps),
            dma(steps),
            dma(steps),
            dma(steps),
            dma(steps),
            dma(steps),
            dma(steps),
            dma(steps),
            dma((NZ,)),
            dma((NZ,)),
            dma((NX,)),
            dma((NX,)),
            dma,
            dma,
            dma((NX,)),
            dma((NX,)),
        ],
        compiler_params=pltpu.CompilerParams(
            collective_id=0, has_side_effects=True, vmem_limit_bytes=40 * 1024 * 1024
        ),
        name="exchange",
    )(step, plan, rate, context, cotangent, weights[0], moment_one[0], moment_two[0], outer)

    wide = n // GRID
    column = pl.BlockSpec((ROWS, wide), lambda i: (0, i))

    def whole(shape):
        return pl.BlockSpec(shape, lambda i: (0,) * len(shape))

    layer_out, context_grad, weights_out, outer_new, momentum_new = pl.pallas_call(
        apply_kernel,
        grid=(GRID,),
        out_shape=(
            jax.ShapeDtypeStruct((ROWS, TOK), bf16),
            jax.ShapeDtypeStruct((ROWS, TOK), bf16),
            jax.ShapeDtypeStruct((ROWS, n), f32),
            jax.ShapeDtypeStruct((ROWS, n), f32),
            jax.ShapeDtypeStruct((ROWS, n), f32),
        ),
        in_specs=[
            smem,
            smem,
            whole((2, ROWS, HALF)),
            whole((ROWS, TOK)),
            whole((NX * QUARTER, HALF)),
            column,
            column,
            column,
        ],
        out_specs=(whole((ROWS, TOK)), whole((ROWS, TOK)), column, column, column),
        compiler_params=pltpu.CompilerParams(vmem_limit_bytes=24 * 1024 * 1024),
        name="apply",
    )(step, plan, lo, cg, sync, stepped, outer, momentum)
    return (layer_out, context_grad, weights_out[None], outer_new, momentum_new)


def solution(mesh):
    return jax.shard_map(
        per_device,
        mesh=mesh,
        in_specs=(
            P("fsdp", "island"),
            P("fsdp", "island"),
            P("island", "fsdp", None),
            P("island", "fsdp", None),
            P("island", "fsdp", None),
            P("fsdp", None),
            P("fsdp", None),
            P(),
            P(),
        ),
        out_specs=(
            P("fsdp", "island"),
            P("fsdp", "island"),
            P("island", "fsdp", None),
            P("fsdp", None),
            P("fsdp", None),
        ),
        check_vma=False,
    )
```

```python
import functools
import math

import jax
import jax.numpy as jnp
from jax import lax
from jax.experimental import pallas as pl
from jax.experimental.pallas import tpu as pltpu
from jax.sharding import PartitionSpec as P

FRAGMENTS = 4

beta_one = 0.9
beta_two = 0.95
inner_rate = 0.01
weight_decay = 0.1
epsilon = 1e-08
outer_rate = 0.7
momentum_keep = 0.9
period_steps = 4096.0

NY, NZ, NX = 8, 8, 4
ROWS = 40
PAD = 48
UNIT = 80
CHUNK = NZ * UNIT
TOK = 256
HALF = 128
BLOCKS = 40
CHOSEN = 10
VMEM_LIMIT = 64 * 1024 * 1024
QUARTER = 112

f32 = jnp.float32
bf16 = jnp.bfloat16
MESH = pl.DeviceIdType.MESH


def loop(count, body):
    def step(i, carry):
        body(i)
        return carry

    lax.fori_loop(0, count, step, 0)


def exchange_kernel(
    step_s,
    plan_s,
    rate_s,
    ctx_h,
    cot_h,
    w_h,
    m1_h,
    m2_h,
    outer_h,
    lo_o,
    cg_o,
    stepped_o,
    sync_o,
    ctx_v,
    cot_v,
    w_v,
    m1_v,
    m2_v,
    outer_v,
    stepped_v,
    cots,
    chip80,
    ctxs,
    ctx96,
    ctxp,
    w96,
    coth,
    part,
    rr,
    rl,
    sr,
    sl,
    zbuf,
    zrec,
    acc,
    diff,
    gath,
    xs,
    xr,
    zhs,
    zhr,
    fin,
    keep,
    given,
    in_sem,
    sib_s,
    sib_r,
    chs,
    chr_,
    azs,
    azr,
    ars,
    arr,
    als,
    alr,
    rrs,
    rrr,
    rls,
    rlr,
    rzs,
    rzr,
    xss,
    xsr,
    zh_s,
    zh_r,
    xas,
    xar,
):
    fs = lax.axis_index("fsdp")
    isl = lax.axis_index("island")
    c = lax.rem(fs, 2)
    o = 1 - c
    z = lax.rem(lax.div(fs, 2), NZ)
    y = lax.div(fs, 2 * NZ)
    x = lax.rem(isl, NX)
    zh = lax.div(isl, NX)

    turn = [lax.rem(y + k, NY) for k in range(NY)]

    code = jnp.int32(0)
    for k in range(NZ):
        near = sorted(range(NZ), key=lambda u: (abs(u - k), u))
        digits = sum(u * 8**i for i, u in enumerate(near))
        code = code + digits * (1 - lax.div((z - k) * (z - k) + 63, 64))
    order = [lax.rem(lax.div(code, 8**p), 8) for p in range(NZ)]

    def dev(yy, zz, cc):
        return ((yy * NZ + zz) * 2 + cc, isl)

    sibling = dev(y, z, o)
    right = dev(turn[1], z, c)
    left = dev(turn[NY - 1], z, c)

    def xdev(d):
        return (fs, zh * NX + lax.rem(x + d, NX))

    zhdev = (fs, (1 - zh) * NX + x)

    def remote(src, dst, send, recv, device):
        return pltpu.make_async_remote_copy(
            src_ref=src,
            dst_ref=dst,
            send_sem=send,
            recv_sem=recv,
            device_id=device,
            device_id_type=MESH,
        )

    loads = [
        pltpu.make_async_copy(src, dst, in_sem.at[i])
        for i, (src, dst) in enumerate(
            (
                (cot_h, cot_v),
                (ctx_h, ctx_v),
                (w_h, w_v),
                (m1_h, m1_v),
                (m2_h, m2_v),
                (outer_h, outer_v),
            )
        )
    ]
    for load in loads:
        load.start()

    barrier = pltpu.get_barrier_semaphore()

    def greet(device):
        pl.semaphore_signal(barrier, inc=1, device_id=device, device_id_type=MESH)

    greet(zhdev)
    for p in range(NZ - 1, 0, -1):
        greet(dev(y, order[p], c))
    for d in range(1, NX):
        greet(xdev(d))
    greet(right)
    greet(left)
    greet(sibling)

    mine40 = pl.ds(pl.multiple_of(c * ROWS, 8), ROWS)
    other40 = pl.ds(pl.multiple_of(o * ROWS, 8), ROWS)
    mine48 = pl.ds(pl.multiple_of(c * PAD, 16), PAD)
    other48 = pl.ds(pl.multiple_of(o * PAD, 16), PAD)

    loads[0].wait()
    for h in range(2):
        cots[h] = cot_v[:, h * HALF : (h + 1) * HALF].astype(f32)
    chip80[mine40, :] = cots[c]

    loads[1].wait()
    wide = jnp.concatenate([ctx_v[...].astype(f32), jnp.zeros((PAD - ROWS, TOK), f32)], axis=0)
    wide = wide.astype(bf16)
    ctxp[...] = wide
    for h in range(2):
        ctxs[h] = wide[:, h * HALF : (h + 1) * HALF]
    ctx96[mine48, :] = ctxs[c]

    loads[2].wait()

    def half_weights(i):
        lanes = pl.ds(pl.multiple_of(i * CHUNK, 128), CHUNK)
        rows = jnp.concatenate([w_v[:, lanes], jnp.zeros((PAD - ROWS, CHUNK), f32)], axis=0)
        w96[mine48, lanes] = rows.astype(bf16)

    loop(NY, half_weights)

    pl.semaphore_wait(barrier, 3 + NZ - 1 + NX - 1 + 1)

    sib_cot = remote(cots.at[o], chip80.at[mine40], sib_s.at[0], sib_r.at[0], sibling)
    sib_cot.start()
    sib_ctx = remote(ctxs.at[o], ctx96.at[mine48], sib_s.at[1], sib_r.at[1], sibling)
    sib_ctx.start()
    sib_w = remote(w96.at[mine48], w96.at[mine48], sib_s.at[2], sib_r.at[2], sibling)
    sib_w.start()

    def ag_z_send(p):
        ref = coth.at[c, y, z]
        return remote(ref, ref, azs.at[order[p]], azr.at[z], dev(y, order[p], c))

    def ag_z_recv(p):
        ref = coth.at[c, y, order[p]]
        return remote(ref, ref, azs.at[order[p]], azr.at[order[p]], dev(y, order[p], c))

    def ag_y(s, p, sign, landed):
        ref = coth.at[c, turn[(-sign * (s + landed)) % NY], order[p]]
        if sign > 0:
            return remote(ref, ref, ars.at[s, p], arr.at[s, p], right)
        return remote(ref, ref, als.at[s, p], alr.at[s, p], left)

    def ways(p):
        return ((1, 4 - p % 2), (-1, 3 + p % 2))

    def ag(s, *units):
        for p in units:
            if s == 0 and p > 0:
                ag_z_recv(p).wait_recv()
            for sign, hops in ways(p):
                if 0 < s <= hops:
                    ag_y(s - 1, p, sign, 1).wait_recv()
                if s < hops:
                    ag_y(s, p, sign, 0).start()

    def chunk_copy(k, yc):
        ref = coth.at[c, yc]
        return remote(ref, ref, chs.at[k], chr_.at[k], sibling)

    def chunk_recv(k, yc):
        ref = coth.at[o, yc]
        return remote(ref, ref, chs.at[k], chr_.at[k], sibling)

    remote(cots.at[o], chip80.at[other40], sib_s.at[0], sib_r.at[0], sibling).wait_recv()
    coth[c, y, z] = chip80[...].astype(bf16)
    for p in range(1, NZ):
        ag_z_send(p).start()
    ag(0, 0)

    remote(ctxs.at[o], ctx96.at[other48], sib_s.at[1], sib_r.at[1], sibling).wait_recv()
    remote(w96.at[mine48], w96.at[other48], sib_s.at[2], sib_r.at[2], sibling).wait_recv()

    def partial_out(i):
        lanes = pl.ds(pl.multiple_of(i * CHUNK, 128), CHUNK)
        total = lax.dot_general(
            w96[:, lanes], ctx96[...], (((0,), (0,)), ((), ())), preferred_element_type=f32
        )
        part[i] = total.reshape(NZ, UNIT, HALF)

    loop(NY, partial_out)

    far, near = (7, 6, 5, 4), (3, 2, 1, 0)

    def rs_copy(s, p, sign):
        if sign > 0:
            return remote(sr.at[s, p], rr.at[s, p], rrs.at[s, p], rrr.at[s, p], right)
        return remote(sl.at[s, p], rl.at[s, p], rls.at[s, p], rlr.at[s, p], left)

    def rs(s, units):
        for p in units:
            for sign, hops in ways(p):
                if s < hops:
                    value = part[turn[(sign * (hops - s)) % NY], order[p]]
                    if s > 0:
                        rs_copy(s - 1, p, sign).wait_recv()
                        came = rr if sign > 0 else rl
                        value = value + came[s - 1, p].astype(f32)
                    going = sr if sign > 0 else sl
                    going[s, p] = value.astype(bf16)
                    rs_copy(s, p, sign).start()

    def rs_z(p):
        return remote(
            zbuf.at[p], zrec.at[z], rzs.at[p], rzr.at[z], dev(y, order[p], c)
        )

    def rs_z_recv(p):
        return remote(
            zbuf.at[p], zrec.at[order[p]], rzs.at[p], rzr.at[order[p]], dev(y, order[p], c)
        )

    def rs_last(units):
        for p in units:
            value = part[y, order[p]]
            for sign, hops in ways(p):
                rs_copy(hops - 1, p, sign).wait_recv()
                came = rr if sign > 0 else rl
                value = value + came[hops - 1, p].astype(f32)
            if p == 0:
                keep[...] = value
            else:
                zbuf[p] = value.astype(bf16)
                rs_z(p).start()

    acc[...] = jnp.zeros_like(acc)
    rate = rate_s[0]

    def compute(k, yc):
        chunk_recv(k, yc).wait_recv()
        lanes = pl.ds(pl.multiple_of(yc * CHUNK, 128), CHUNK)
        incoming = jnp.concatenate(
            [coth[0, yc].reshape(CHUNK, HALF), coth[1, yc].reshape(CHUNK, HALF)], axis=1
        )
        acc[...] += jnp.dot(w96[mine48, lanes], incoming, preferred_element_type=f32)
        grad = lax.dot_general(
            ctxp[...], incoming, (((1,), (1,)), ((), ())), preferred_element_type=f32
        )[:ROWS]
        master = w_v[:, lanes]
        first = beta_one * m1_v[:, lanes].astype(f32) + (1.0 - beta_one) * grad
        second = beta_two * m2_v[:, lanes].astype(f32) + (1.0 - beta_two) * grad * grad
        stepped = master - rate * (first / (jnp.sqrt(second) + epsilon) + weight_decay * master)
        stepped_v[:, lanes] = stepped
        delta = outer_v[:, lanes] - stepped
        for b in range(CHUNK // HALF):
            diff[yc * (CHUNK // HALF) + b] = delta[:, b * HALF : (b + 1) * HALF]

    def compute_pair(s):
        def body(i):
            compute(2 * s - 1 + i, lax.rem(y + NY + (2 * i - 1) * s, NY))

        loop(2, body)

    def share_pair(s):
        chunk_copy(2 * s - 1, turn[NY - s]).start()
        chunk_copy(2 * s, turn[s]).start()

    rs(0, far)
    ag(0, 1, 2)
    ag(1, 0)
    rs(0, near)
    ag(0, 3, 4)
    ag(1, 1, 2)
    ag(2, 0)
    ag(0, 5, 6)
    ag(1, 3, 4)
    ag(2, 1, 2)
    ag(3, 0)
    ag(0, 7)
    chunk_copy(0, y).start()
    rs(1, far)
    ag(1, 5, 6)
    ag(2, 3, 4)
    ag(3, 1, 2)
    for i in range(3, 6):
        loads[i].wait()
    compute(0, y)
    ag(1, 7)
    share_pair(1)
    ag(2, 5, 6)
    ag(3, 3, 4)
    compute_pair(1)
    ag(2, 7)
    share_pair(2)
    rs(1, near)
    ag(3, 5, 6)
    compute_pair(2)
    ag(3, 7)
    share_pair(3)
    rs(2, far)
    compute_pair(3)
    ag(4, *range(NZ))
    chunk_copy(7, turn[4]).start()

    current = lax.rem(step_s[0], FRAGMENTS)

    def rank(b, carry):
        count, found = carry[0], carry[1:]
        hit = plan_s[b] == current
        found = tuple(jnp.where(hit & (count == i), b, e) for i, e in enumerate(found))
        return (count + hit.astype(jnp.int32),) + found

    ranked = lax.fori_loop(0, BLOCKS, rank, (jnp.int32(0),) * (CHOSEN + 1))
    chosen = ranked[1:]

    compute(7, turn[4])
    for i in range(CHOSEN):
        gath[i * ROWS : (i + 1) * ROWS, :] = diff[chosen[i]]
    gath[CHOSEN * ROWS :, :] = jnp.zeros((NX * QUARTER - CHOSEN * ROWS, HALF), f32)
    xs[...] = gath[...].astype(bf16).reshape(NX, QUARTER, HALF)

    def x_scatter(d):
        return remote(xs.at[lax.rem(x + d, NX)], xr.at[d], xss.at[d], xsr.at[d], xdev(d))

    def x_gather(d):
        return remote(fin.at[x], fin.at[x], xas.at[d], xar.at[d], xdev(d))

    def x_gathered(d):
        ref = fin.at[lax.rem(x + NX - d, NX)]
        return remote(ref, ref, xas.at[d], xar.at[d], xdev(d))

    for d in (2, 1, 3):
        x_scatter(d).start()
    save = pltpu.make_async_copy(stepped_v, stepped_o, in_sem.at[6])
    save.start()
    cg_o[...] = acc[:ROWS, :]
    rs(2, near)
    for d in range(1, NX):
        x_scatter(d).wait_recv()
    total = xs[x].astype(f32)
    for d in range(1, NX):
        total = total + xr[d].astype(f32)
    zhs[...] = total.astype(bf16)
    across = remote(zhs, zhr, zh_s, zh_r, zhdev)
    across.start()
    rs(3, far)
    rs(3, near)
    rs_last(far)
    rs_last(near)
    across.wait_recv()
    fin[x] = (zhs[...].astype(f32) + zhr[...].astype(f32)).astype(bf16)
    for d in (2, 1, 3):
        x_gather(d).start()

    sib_cot.wait_send()
    sib_ctx.wait_send()
    sib_w.wait_send()
    for p in range(1, NZ):
        ag_z_send(p).wait_send()
    for p in range(NZ):
        for sign, hops in ways(p):
            for s in range(hops):
                ag_y(s, p, sign, 0).wait_send()
                rs_copy(s, p, sign).wait_send()
    chunk_copy(0, y).wait_send()
    for s in range(1, 4):
        chunk_copy(2 * s - 1, turn[NY - s]).wait_send()
        chunk_copy(2 * s, turn[s]).wait_send()
    chunk_copy(7, turn[4]).wait_send()
    for d in range(1, NX):
        x_scatter(d).wait_send()
    across.wait_send()
    save.wait()

    value = keep[...]
    for p in range(1, NZ):
        rs_z_recv(p).wait_recv()
        value = value + zrec[order[p]].astype(f32)
    keep[...] = value
    give = remote(keep.at[other40], given, sib_s.at[3], sib_r.at[3], sibling)
    give.start()
    lo_o[c] = keep[mine40, :]
    for p in range(1, NZ):
        rs_z(p).wait_send()
    for d in range(1, NX):
        x_gathered(d).wait_recv()
    sync_o[...] = fin[...].reshape(NX * QUARTER, HALF).astype(f32)
    give.wait_recv()
    lo_o[o] = given[...]
    give.wait_send()
    for d in range(1, NX):
        x_gather(d).wait_send()


GRID = 2


def apply_kernel(
    step_s,
    plan_s,
    lo_i,
    cg_i,
    sync_i,
    stepped_i,
    outer_i,
    mom_i,
    lo_o,
    cg_o,
    w_o,
    outer_o,
    mom_o,
):
    tile = pl.program_id(0)
    per = BLOCKS // GRID

    @pl.when(tile == 0)
    def _():
        for h in range(2):
            lo_o[:, h * HALF : (h + 1) * HALF] = lo_i[h].astype(bf16)
        cg_o[...] = cg_i[...].astype(bf16)

    current = lax.rem(step_s[0], FRAGMENTS)

    def before(b, count):
        return count + (plan_s[b] == current).astype(jnp.int32)

    count = lax.fori_loop(0, tile * per, before, jnp.int32(0))
    for b in range(per):
        lanes = slice(b * HALF, (b + 1) * HALF)
        hit = plan_s[tile * per + b] == current
        slot = jnp.minimum(count, CHOSEN - 1)
        pseudo = sync_i[pl.ds(pl.multiple_of(slot * ROWS, 8), ROWS), :] / 8.0
        count = count + hit.astype(jnp.int32)
        old, mom = outer_i[:, lanes], mom_i[:, lanes]
        mom_next = momentum_keep * mom + pseudo
        new = old - outer_rate * (pseudo + momentum_keep * mom_next)
        mom_o[:, lanes] = jnp.where(hit, mom_next, mom)
        outer_o[:, lanes] = jnp.where(hit, new, old)
        w_o[:, lanes] = jnp.where(hit, new, stepped_i[:, lanes])


def per_device(context, cotangent, weights, moment_one, moment_two, outer, momentum, step, plan):
    n = outer.shape[1]
    rate = inner_rate * (0.55 + 0.45 * jnp.cos(math.pi * step.astype(f32) / period_steps))
    smem = pl.BlockSpec(memory_space=pltpu.SMEM)
    vmem = pl.BlockSpec(memory_space=pltpu.VMEM)
    hbm = pl.BlockSpec(memory_space=pltpu.HBM)
    dma = pltpu.SemaphoreType.DMA
    steps = (4, NZ)
    lo, cg, stepped, sync = pl.pallas_call(
        exchange_kernel,
        out_shape=(
            jax.ShapeDtypeStruct((2, ROWS, HALF), f32),
            jax.ShapeDtypeStruct((ROWS, TOK), f32),
            jax.ShapeDtypeStruct((ROWS, n), f32),
            jax.ShapeDtypeStruct((NX * QUARTER, HALF), f32),
        ),
        in_specs=[smem] * 3 + [hbm] * 6,
        out_specs=(vmem, vmem, hbm, vmem),
        scratch_shapes=[
            pltpu.VMEM((ROWS, TOK), bf16),
            pltpu.VMEM((ROWS, TOK), bf16),
            pltpu.VMEM((ROWS, n), f32),
            pltpu.VMEM((ROWS, n), bf16),
            pltpu.VMEM((ROWS, n), bf16),
            pltpu.VMEM((ROWS, n), f32),
            pltpu.VMEM((ROWS, n), f32),
            pltpu.VMEM((2, ROWS, HALF), f32),
            pltpu.VMEM((UNIT, HALF), f32),
            pltpu.VMEM((2, PAD, HALF), bf16),
            pltpu.VMEM((2 * PAD, HALF), bf16),
            pltpu.VMEM((PAD, TOK), bf16),
            pltpu.VMEM((2 * PAD, n), bf16),
            pltpu.VMEM((2, NY, NZ, UNIT, HALF), bf16),
            pltpu.VMEM((NY, NZ, UNIT, HALF), f32),
            pltpu.VMEM(steps + (UNIT, HALF), bf16),
            pltpu.VMEM(steps + (UNIT, HALF), bf16),
            pltpu.VMEM(steps + (UNIT, HALF), bf16),
            pltpu.VMEM(steps + (UNIT, HALF), bf16),
            pltpu.VMEM((NZ, UNIT, HALF), bf16),
            pltpu.VMEM((NZ, UNIT, HALF), bf16),
            pltpu.VMEM((PAD, TOK), f32),
            pltpu.VMEM((BLOCKS, ROWS, HALF), f32),
            pltpu.VMEM((NX * QUARTER, HALF), f32),
            pltpu.VMEM((NX, QUARTER, HALF), bf16),
            pltpu.VMEM((NX, QUARTER, HALF), bf16),
            pltpu.VMEM((QUARTER, HALF), bf16),
            pltpu.VMEM((QUARTER, HALF), bf16),
            pltpu.VMEM((NX, QUARTER, HALF), bf16),
            pltpu.VMEM((UNIT, HALF), f32),
            pltpu.VMEM((ROWS, HALF), f32),
            dma((7,)),
            dma((4,)),
            dma((4,)),
            dma((NY,)),
            dma((NY,)),
            dma((NZ,)),
            dma((NZ,)),
            dma(steps),
            dma(steps),
            dma(steps),
            dma(steps),
            dma(steps),
            dma(steps),
            dma(steps),
            dma(steps),
            dma((NZ,)),
            dma((NZ,)),
            dma((NX,)),
            dma((NX,)),
            dma,
            dma,
            dma((NX,)),
            dma((NX,)),
        ],
        compiler_params=pltpu.CompilerParams(
            collective_id=0, has_side_effects=True, vmem_limit_bytes=VMEM_LIMIT
        ),
        name="exchange",
    )(step, plan, rate, context, cotangent, weights[0], moment_one[0], moment_two[0], outer)

    wide = n // GRID
    column = pl.BlockSpec((ROWS, wide), lambda i: (0, i))

    def whole(shape):
        return pl.BlockSpec(shape, lambda i: (0,) * len(shape))

    layer_out, context_grad, weights_out, outer_new, momentum_new = pl.pallas_call(
        apply_kernel,
        grid=(GRID,),
        out_shape=(
            jax.ShapeDtypeStruct((ROWS, TOK), bf16),
            jax.ShapeDtypeStruct((ROWS, TOK), bf16),
            jax.ShapeDtypeStruct((ROWS, n), f32),
            jax.ShapeDtypeStruct((ROWS, n), f32),
            jax.ShapeDtypeStruct((ROWS, n), f32),
        ),
        in_specs=[
            smem,
            smem,
            whole((2, ROWS, HALF)),
            whole((ROWS, TOK)),
            whole((NX * QUARTER, HALF)),
            column,
            column,
            column,
        ],
        out_specs=(whole((ROWS, TOK)), whole((ROWS, TOK)), column, column, column),
        compiler_params=pltpu.CompilerParams(vmem_limit_bytes=VMEM_LIMIT),
        name="apply",
    )(step, plan, lo, cg, sync, stepped, outer, momentum)
    return (layer_out, context_grad, weights_out[None], outer_new, momentum_new)


def solution(mesh):
    return jax.shard_map(
        per_device,
        mesh=mesh,
        in_specs=(
            P("fsdp", "island"),
            P("fsdp", "island"),
            P("island", "fsdp", None),
            P("island", "fsdp", None),
            P("island", "fsdp", None),
            P("fsdp", None),
            P("fsdp", None),
            P(),
            P(),
        ),
        out_specs=(
            P("fsdp", "island"),
            P("fsdp", "island"),
            P("island", "fsdp", None),
            P("fsdp", None),
            P("fsdp", None),
        ),
        check_vma=False,
    )
```

```python
import functools
import math

import jax
import jax.numpy as jnp
from jax import lax
from jax.experimental import pallas as pl
from jax.experimental.pallas import tpu as pltpu
from jax.sharding import PartitionSpec as P

FRAGMENTS = 4

beta_one = 0.9
beta_two = 0.95
inner_rate = 0.01
weight_decay = 0.1
epsilon = 1e-08
outer_rate = 0.7
momentum_keep = 0.9
period_steps = 4096.0

NY, NZ, NX = 8, 8, 4
ROWS = 40
PAD = 48
UNIT = 80
CHUNK = NZ * UNIT
TOK = 256
HALF = 128
BLOCKS = 40
CHOSEN = 10
VMEM_LIMIT = 64 * 1024 * 1024
QUARTER = 112

f32 = jnp.float32
bf16 = jnp.bfloat16
MESH = pl.DeviceIdType.MESH


def loop(count, body):
    def step(i, carry):
        body(i)
        return carry

    lax.fori_loop(0, count, step, 0)


def exchange_kernel(
    step_s,
    plan_s,
    rate_s,
    ctx_h,
    cot_h,
    w_h,
    m1_h,
    m2_h,
    outer_h,
    lo_o,
    cg_o,
    stepped_o,
    sync_o,
    ctx_v,
    cot_v,
    w_v,
    m1_v,
    m2_v,
    outer_v,
    stepped_v,
    cots,
    chip80,
    ctxs,
    ctx96,
    ctxp,
    w96,
    coth,
    part,
    rr,
    rl,
    sr,
    sl,
    zbuf,
    zrec,
    acc,
    diff,
    gath,
    xs,
    xr,
    zhs,
    zhr,
    fin,
    keep,
    given,
    in_sem,
    sib_s,
    sib_r,
    chs,
    chr_,
    azs,
    azr,
    ars,
    arr,
    als,
    alr,
    rrs,
    rrr,
    rls,
    rlr,
    rzs,
    rzr,
    xss,
    xsr,
    zh_s,
    zh_r,
    xas,
    xar,
):
    fs = lax.axis_index("fsdp")
    isl = lax.axis_index("island")
    c = lax.rem(fs, 2)
    o = 1 - c
    z = lax.rem(lax.div(fs, 2), NZ)
    y = lax.div(fs, 2 * NZ)
    x = lax.rem(isl, NX)
    zh = lax.div(isl, NX)

    turn = [lax.rem(y + k, NY) for k in range(NY)]

    code = jnp.int32(0)
    for k in range(NZ):
        near = sorted(range(NZ), key=lambda u: (abs(u - k), u))
        digits = sum(u * 8**i for i, u in enumerate(near))
        code = code + digits * (1 - lax.div((z - k) * (z - k) + 63, 64))
    order = [lax.rem(lax.div(code, 8**p), 8) for p in range(NZ)]

    def dev(yy, zz, cc):
        return ((yy * NZ + zz) * 2 + cc, isl)

    sibling = dev(y, z, o)
    right = dev(turn[1], z, c)
    left = dev(turn[NY - 1], z, c)

    def xdev(d):
        return (fs, zh * NX + lax.rem(x + d, NX))

    zhdev = (fs, (1 - zh) * NX + x)

    def remote(src, dst, send, recv, device):
        return pltpu.make_async_remote_copy(
            src_ref=src,
            dst_ref=dst,
            send_sem=send,
            recv_sem=recv,
            device_id=device,
            device_id_type=MESH,
        )

    loads = [
        pltpu.make_async_copy(src, dst, in_sem.at[i])
        for i, (src, dst) in enumerate(
            (
                (cot_h, cot_v),
                (ctx_h, ctx_v),
                (w_h, w_v),
                (m1_h, m1_v),
                (m2_h, m2_v),
                (outer_h, outer_v),
            )
        )
    ]
    for load in loads:
        load.start()

    barrier = pltpu.get_barrier_semaphore()

    def greet(device):
        pl.semaphore_signal(barrier, inc=1, device_id=device, device_id_type=MESH)

    greet(zhdev)
    for p in range(NZ - 1, 0, -1):
        greet(dev(y, order[p], c))
    for d in range(1, NX):
        greet(xdev(d))
    greet(right)
    greet(left)
    greet(sibling)

    mine40 = pl.ds(pl.multiple_of(c * ROWS, 8), ROWS)
    other40 = pl.ds(pl.multiple_of(o * ROWS, 8), ROWS)
    mine48 = pl.ds(pl.multiple_of(c * PAD, 16), PAD)
    other48 = pl.ds(pl.multiple_of(o * PAD, 16), PAD)

    loads[0].wait()
    for h in range(2):
        cots[h] = cot_v[:, h * HALF : (h + 1) * HALF].astype(f32)
    chip80[mine40, :] = cots[c]

    loads[1].wait()
    wide = jnp.concatenate([ctx_v[...].astype(f32), jnp.zeros((PAD - ROWS, TOK), f32)], axis=0)
    wide = wide.astype(bf16)
    ctxp[...] = wide
    for h in range(2):
        ctxs[h] = wide[:, h * HALF : (h + 1) * HALF]
    ctx96[mine48, :] = ctxs[c]

    loads[2].wait()

    def half_weights(i):
        lanes = pl.ds(pl.multiple_of(i * CHUNK, 128), CHUNK)
        rows = jnp.concatenate([w_v[:, lanes], jnp.zeros((PAD - ROWS, CHUNK), f32)], axis=0)
        w96[mine48, lanes] = rows.astype(bf16)

    loop(NY, half_weights)

    pl.semaphore_wait(barrier, 3 + NZ - 1 + NX - 1 + 1)

    sib_cot = remote(cots.at[o], chip80.at[mine40], sib_s.at[0], sib_r.at[0], sibling)
    sib_cot.start()
    sib_ctx = remote(ctxs.at[o], ctx96.at[mine48], sib_s.at[1], sib_r.at[1], sibling)
    sib_ctx.start()
    sib_w = remote(w96.at[mine48], w96.at[mine48], sib_s.at[2], sib_r.at[2], sibling)
    sib_w.start()

    def ag_z_send(p):
        ref = coth.at[c, y, z]
        return remote(ref, ref, azs.at[order[p]], azr.at[z], dev(y, order[p], c))

    def ag_z_recv(p):
        ref = coth.at[c, y, order[p]]
        return remote(ref, ref, azs.at[order[p]], azr.at[order[p]], dev(y, order[p], c))

    def ag_y(s, p, sign, landed):
        ref = coth.at[c, turn[(-sign * (s + landed)) % NY], order[p]]
        if sign > 0:
            return remote(ref, ref, ars.at[s, p], arr.at[s, p], right)
        return remote(ref, ref, als.at[s, p], alr.at[s, p], left)

    def ways(p):
        return ((1, 4 - p % 2), (-1, 3 + p % 2))

    def ag(s, *units):
        for p in units:
            if s == 0 and p > 0:
                ag_z_recv(p).wait_recv()
            for sign, hops in ways(p):
                if 0 < s <= hops:
                    ag_y(s - 1, p, sign, 1).wait_recv()
                if s < hops:
                    ag_y(s, p, sign, 0).start()

    def chunk_copy(k, yc):
        ref = coth.at[c, yc]
        return remote(ref, ref, chs.at[k], chr_.at[k], sibling)

    def chunk_recv(k, yc):
        ref = coth.at[o, yc]
        return remote(ref, ref, chs.at[k], chr_.at[k], sibling)

    remote(cots.at[o], chip80.at[other40], sib_s.at[0], sib_r.at[0], sibling).wait_recv()
    coth[c, y, z] = chip80[...].astype(bf16)
    for p in range(1, NZ):
        ag_z_send(p).start()
    ag(0, 0)

    remote(ctxs.at[o], ctx96.at[other48], sib_s.at[1], sib_r.at[1], sibling).wait_recv()
    remote(w96.at[mine48], w96.at[other48], sib_s.at[2], sib_r.at[2], sibling).wait_recv()

    def partial_out(i):
        lanes = pl.ds(pl.multiple_of(i * CHUNK, 128), CHUNK)
        total = lax.dot_general(
            w96[:, lanes], ctx96[...], (((0,), (0,)), ((), ())), preferred_element_type=f32
        )
        part[i] = total.reshape(NZ, UNIT, HALF)

    loop(NY, partial_out)

    far, near = (7, 6, 5, 4), (3, 2, 1, 0)

    def rs_copy(s, p, sign):
        if sign > 0:
            return remote(sr.at[s, p], rr.at[s, p], rrs.at[s, p], rrr.at[s, p], right)
        return remote(sl.at[s, p], rl.at[s, p], rls.at[s, p], rlr.at[s, p], left)

    def rs(s, units):
        for p in units:
            for sign, hops in ways(p):
                if s < hops:
                    value = part[turn[(sign * (hops - s)) % NY], order[p]]
                    if s > 0:
                        rs_copy(s - 1, p, sign).wait_recv()
                        came = rr if sign > 0 else rl
                        value = value + came[s - 1, p].astype(f32)
                    going = sr if sign > 0 else sl
                    going[s, p] = value.astype(bf16)
                    rs_copy(s, p, sign).start()

    def rs_z(p):
        return remote(
            zbuf.at[p], zrec.at[z], rzs.at[p], rzr.at[z], dev(y, order[p], c)
        )

    def rs_z_recv(p):
        return remote(
            zbuf.at[p], zrec.at[order[p]], rzs.at[p], rzr.at[order[p]], dev(y, order[p], c)
        )

    def rs_last(units):
        for p in units:
            value = part[y, order[p]]
            for sign, hops in ways(p):
                rs_copy(hops - 1, p, sign).wait_recv()
                came = rr if sign > 0 else rl
                value = value + came[hops - 1, p].astype(f32)
            if p == 0:
                keep[...] = value
            else:
                zbuf[p] = value.astype(bf16)
                rs_z(p).start()

    acc[...] = jnp.zeros_like(acc)
    rate = rate_s[0]

    def compute(k, yc):
        chunk_recv(k, yc).wait_recv()
        lanes = pl.ds(pl.multiple_of(yc * CHUNK, 128), CHUNK)
        incoming = jnp.concatenate(
            [coth[0, yc].reshape(CHUNK, HALF), coth[1, yc].reshape(CHUNK, HALF)], axis=1
        )
        acc[...] += jnp.dot(w96[mine48, lanes], incoming, preferred_element_type=f32)
        grad = lax.dot_general(
            ctxp[...], incoming, (((1,), (1,)), ((), ())), preferred_element_type=f32
        )[:ROWS]
        master = w_v[:, lanes]
        first = beta_one * m1_v[:, lanes].astype(f32) + (1.0 - beta_one) * grad
        second = beta_two * m2_v[:, lanes].astype(f32) + (1.0 - beta_two) * grad * grad
        stepped = master - rate * (first / (jnp.sqrt(second) + epsilon) + weight_decay * master)
        stepped_v[:, lanes] = stepped
        delta = outer_v[:, lanes] - stepped
        for b in range(CHUNK // HALF):
            diff[yc * (CHUNK // HALF) + b] = delta[:, b * HALF : (b + 1) * HALF]

    def compute_pair(s):
        def body(i):
            compute(2 * s - 1 + i, lax.rem(y + NY + (2 * i - 1) * s, NY))

        loop(2, body)

    def share_pair(s):
        chunk_copy(2 * s - 1, turn[NY - s]).start()
        chunk_copy(2 * s, turn[s]).start()

    rs(0, far)
    ag(0, 1, 2)
    ag(1, 0)
    rs(0, near)
    ag(0, 3, 4)
    ag(1, 1, 2)
    ag(2, 0)
    ag(0, 5, 6)
    ag(1, 3, 4)
    ag(2, 1, 2)
    ag(3, 0)
    ag(0, 7)
    chunk_copy(0, y).start()
    rs(1, far)
    ag(1, 5, 6)
    ag(2, 3, 4)
    ag(3, 1, 2)
    for i in range(3, 6):
        loads[i].wait()
    compute(0, y)
    ag(1, 7)
    share_pair(1)
    ag(2, 5, 6)
    ag(3, 3, 4)
    compute_pair(1)
    ag(2, 7)
    share_pair(2)
    rs(1, near)
    ag(3, 5, 6)
    compute_pair(2)
    ag(3, 7)
    share_pair(3)
    rs(2, far)
    compute_pair(3)
    rs(2, near)
    ag(4, *range(NZ))
    chunk_copy(7, turn[4]).start()

    current = lax.rem(step_s[0], FRAGMENTS)

    def rank(b, carry):
        count, found = carry[0], carry[1:]
        hit = plan_s[b] == current
        found = tuple(jnp.where(hit & (count == i), b, e) for i, e in enumerate(found))
        return (count + hit.astype(jnp.int32),) + found

    ranked = lax.fori_loop(0, BLOCKS, rank, (jnp.int32(0),) * (CHOSEN + 1))
    chosen = ranked[1:]

    compute(7, turn[4])
    for i in range(CHOSEN):
        gath[i * ROWS : (i + 1) * ROWS, :] = diff[chosen[i]]
    gath[CHOSEN * ROWS :, :] = jnp.zeros((NX * QUARTER - CHOSEN * ROWS, HALF), f32)
    xs[...] = gath[...].astype(bf16).reshape(NX, QUARTER, HALF)

    def x_scatter(d):
        return remote(xs.at[lax.rem(x + d, NX)], xr.at[d], xss.at[d], xsr.at[d], xdev(d))

    def x_gather(d):
        return remote(fin.at[x], fin.at[x], xas.at[d], xar.at[d], xdev(d))

    def x_gathered(d):
        ref = fin.at[lax.rem(x + NX - d, NX)]
        return remote(ref, ref, xas.at[d], xar.at[d], xdev(d))

    for d in (2, 1, 3):
        x_scatter(d).start()
    save = pltpu.make_async_copy(stepped_v, stepped_o, in_sem.at[6])
    save.start()
    cg_o[...] = acc[:ROWS, :]
    rs(3, far)
    for d in range(1, NX):
        x_scatter(d).wait_recv()
    total = xs[x].astype(f32)
    for d in range(1, NX):
        total = total + xr[d].astype(f32)
    zhs[...] = total.astype(bf16)
    across = remote(zhs, zhr, zh_s, zh_r, zhdev)
    across.start()
    rs(3, near)
    rs_last(far)
    rs_last(near)
    across.wait_recv()
    fin[x] = (zhs[...].astype(f32) + zhr[...].astype(f32)).astype(bf16)
    for d in (2, 1, 3):
        x_gather(d).start()

    sib_cot.wait_send()
    sib_ctx.wait_send()
    sib_w.wait_send()
    for p in range(1, NZ):
        ag_z_send(p).wait_send()
    for p in range(NZ):
        for sign, hops in ways(p):
            for s in range(hops):
                ag_y(s, p, sign, 0).wait_send()
                rs_copy(s, p, sign).wait_send()
    chunk_copy(0, y).wait_send()
    for s in range(1, 4):
        chunk_copy(2 * s - 1, turn[NY - s]).wait_send()
        chunk_copy(2 * s, turn[s]).wait_send()
    chunk_copy(7, turn[4]).wait_send()
    for d in range(1, NX):
        x_scatter(d).wait_send()
    across.wait_send()
    save.wait()

    value = keep[...]
    for p in range(1, NZ):
        rs_z_recv(p).wait_recv()
        value = value + zrec[order[p]].astype(f32)
    keep[...] = value
    give = remote(keep.at[other40], given, sib_s.at[3], sib_r.at[3], sibling)
    give.start()
    lo_o[c] = keep[mine40, :]
    for p in range(1, NZ):
        rs_z(p).wait_send()
    for d in range(1, NX):
        x_gathered(d).wait_recv()
    sync_o[...] = fin[...].reshape(NX * QUARTER, HALF).astype(f32)
    give.wait_recv()
    lo_o[o] = given[...]
    give.wait_send()
    for d in range(1, NX):
        x_gather(d).wait_send()


GRID = 2


def apply_kernel(
    step_s,
    plan_s,
    lo_i,
    cg_i,
    sync_i,
    stepped_i,
    outer_i,
    mom_i,
    lo_o,
    cg_o,
    w_o,
    outer_o,
    mom_o,
):
    tile = pl.program_id(0)
    per = BLOCKS // GRID

    @pl.when(tile == 0)
    def _():
        for h in range(2):
            lo_o[:, h * HALF : (h + 1) * HALF] = lo_i[h].astype(bf16)
        cg_o[...] = cg_i[...].astype(bf16)

    current = lax.rem(step_s[0], FRAGMENTS)

    def before(b, count):
        return count + (plan_s[b] == current).astype(jnp.int32)

    count = lax.fori_loop(0, tile * per, before, jnp.int32(0))
    for b in range(per):
        lanes = slice(b * HALF, (b + 1) * HALF)
        hit = plan_s[tile * per + b] == current
        slot = jnp.minimum(count, CHOSEN - 1)
        pseudo = sync_i[pl.ds(pl.multiple_of(slot * ROWS, 8), ROWS), :] / 8.0
        count = count + hit.astype(jnp.int32)
        old, mom = outer_i[:, lanes], mom_i[:, lanes]
        mom_next = momentum_keep * mom + pseudo
        new = old - outer_rate * (pseudo + momentum_keep * mom_next)
        mom_o[:, lanes] = jnp.where(hit, mom_next, mom)
        outer_o[:, lanes] = jnp.where(hit, new, old)
        w_o[:, lanes] = jnp.where(hit, new, stepped_i[:, lanes])


def per_device(context, cotangent, weights, moment_one, moment_two, outer, momentum, step, plan):
    n = outer.shape[1]
    rate = inner_rate * (0.55 + 0.45 * jnp.cos(math.pi * step.astype(f32) / period_steps))
    smem = pl.BlockSpec(memory_space=pltpu.SMEM)
    vmem = pl.BlockSpec(memory_space=pltpu.VMEM)
    hbm = pl.BlockSpec(memory_space=pltpu.HBM)
    dma = pltpu.SemaphoreType.DMA
    steps = (4, NZ)
    lo, cg, stepped, sync = pl.pallas_call(
        exchange_kernel,
        out_shape=(
            jax.ShapeDtypeStruct((2, ROWS, HALF), f32),
            jax.ShapeDtypeStruct((ROWS, TOK), f32),
            jax.ShapeDtypeStruct((ROWS, n), f32),
            jax.ShapeDtypeStruct((NX * QUARTER, HALF), f32),
        ),
        in_specs=[smem] * 3 + [hbm] * 6,
        out_specs=(vmem, vmem, hbm, vmem),
        scratch_shapes=[
            pltpu.VMEM((ROWS, TOK), bf16),
            pltpu.VMEM((ROWS, TOK), bf16),
            pltpu.VMEM((ROWS, n), f32),
            pltpu.VMEM((ROWS, n), bf16),
            pltpu.VMEM((ROWS, n), bf16),
            pltpu.VMEM((ROWS, n), f32),
            pltpu.VMEM((ROWS, n), f32),
            pltpu.VMEM((2, ROWS, HALF), f32),
            pltpu.VMEM((UNIT, HALF), f32),
            pltpu.VMEM((2, PAD, HALF), bf16),
            pltpu.VMEM((2 * PAD, HALF), bf16),
            pltpu.VMEM((PAD, TOK), bf16),
            pltpu.VMEM((2 * PAD, n), bf16),
            pltpu.VMEM((2, NY, NZ, UNIT, HALF), bf16),
            pltpu.VMEM((NY, NZ, UNIT, HALF), f32),
            pltpu.VMEM(steps + (UNIT, HALF), bf16),
            pltpu.VMEM(steps + (UNIT, HALF), bf16),
            pltpu.VMEM(steps + (UNIT, HALF), bf16),
            pltpu.VMEM(steps + (UNIT, HALF), bf16),
            pltpu.VMEM((NZ, UNIT, HALF), bf16),
            pltpu.VMEM((NZ, UNIT, HALF), bf16),
            pltpu.VMEM((PAD, TOK), f32),
            pltpu.VMEM((BLOCKS, ROWS, HALF), f32),
            pltpu.VMEM((NX * QUARTER, HALF), f32),
            pltpu.VMEM((NX, QUARTER, HALF), bf16),
            pltpu.VMEM((NX, QUARTER, HALF), bf16),
            pltpu.VMEM((QUARTER, HALF), bf16),
            pltpu.VMEM((QUARTER, HALF), bf16),
            pltpu.VMEM((NX, QUARTER, HALF), bf16),
            pltpu.VMEM((UNIT, HALF), f32),
            pltpu.VMEM((ROWS, HALF), f32),
            dma((7,)),
            dma((4,)),
            dma((4,)),
            dma((NY,)),
            dma((NY,)),
            dma((NZ,)),
            dma((NZ,)),
            dma(steps),
            dma(steps),
            dma(steps),
            dma(steps),
            dma(steps),
            dma(steps),
            dma(steps),
            dma(steps),
            dma((NZ,)),
            dma((NZ,)),
            dma((NX,)),
            dma((NX,)),
            dma,
            dma,
            dma((NX,)),
            dma((NX,)),
        ],
        compiler_params=pltpu.CompilerParams(
            collective_id=0, has_side_effects=True, vmem_limit_bytes=VMEM_LIMIT
        ),
        name="exchange",
    )(step, plan, rate, context, cotangent, weights[0], moment_one[0], moment_two[0], outer)

    wide = n // GRID
    column = pl.BlockSpec((ROWS, wide), lambda i: (0, i))

    def whole(shape):
        return pl.BlockSpec(shape, lambda i: (0,) * len(shape))

    layer_out, context_grad, weights_out, outer_new, momentum_new = pl.pallas_call(
        apply_kernel,
        grid=(GRID,),
        out_shape=(
            jax.ShapeDtypeStruct((ROWS, TOK), bf16),
            jax.ShapeDtypeStruct((ROWS, TOK), bf16),
            jax.ShapeDtypeStruct((ROWS, n), f32),
            jax.ShapeDtypeStruct((ROWS, n), f32),
            jax.ShapeDtypeStruct((ROWS, n), f32),
        ),
        in_specs=[
            smem,
            smem,
            whole((2, ROWS, HALF)),
            whole((ROWS, TOK)),
            whole((NX * QUARTER, HALF)),
            column,
            column,
            column,
        ],
        out_specs=(whole((ROWS, TOK)), whole((ROWS, TOK)), column, column, column),
        compiler_params=pltpu.CompilerParams(vmem_limit_bytes=VMEM_LIMIT),
        name="apply",
    )(step, plan, lo, cg, sync, stepped, outer, momentum)
    return (layer_out, context_grad, weights_out[None], outer_new, momentum_new)


def solution(mesh):
    return jax.shard_map(
        per_device,
        mesh=mesh,
        in_specs=(
            P("fsdp", "island"),
            P("fsdp", "island"),
            P("island", "fsdp", None),
            P("island", "fsdp", None),
            P("island", "fsdp", None),
            P("fsdp", None),
            P("fsdp", None),
            P(),
            P(),
        ),
        out_specs=(
            P("fsdp", "island"),
            P("fsdp", "island"),
            P("island", "fsdp", None),
            P("fsdp", None),
            P("fsdp", None),
        ),
        check_vma=False,
    )
```
